32 devices in a mesh: ka: 16 (over z, y, core), rows: 2 (over x).
Axes of the slice: x: 2, y: 2, z: 4, core: 2. Of those that a mesh axis runs over, the one named last changes fastest.
Arguments:
- amplitudes: float32 [256, 64, 2, 2, 256], P('rows', 'ka'), may hold values from -6 to 6
- conduction_values: float32 [2, 512, 64, 256], P(None, 'rows', 'ka'), may hold values from -0.375 to 0.375
- valence_values: float32 [2, 512, 64, 256], P(None, 'rows', 'ka'), may hold values from -0.375 to 0.375
- screened: float32 [2, 64, 512, 512], P(None, None, 'ka', 'rows'), may hold values from -0.024 to 0.024
- conduction_energy: float32 [256, 64], P('rows', 'ka'), may hold values from 0.5 to 1
- valence_energy: float32 [64, 256], P('ka'), may hold values from -0.5 to 0
- offset_table: int32 [64, 64], replicated, may hold values from 0 to 63, as said below
Outputs:
- applied_once: float32 [256, 64, 2, 2, 256], P('rows', 'ka')
- applied_twice: float32 [256, 64, 2, 2, 256], P('rows', 'ka')
The draws below stay inside these ranges and needn't reach their ends.
Inputs may be any that keep to these rules, and one draw needn't show every extreme that they name: offset_table[k, k2] = 4 * 4 * a + 4 * b + d, where (a, b, d) are the coordinates of the grid point of k-point k minus those of k-point k2, each modulo 4, for a one to one assignment of the 64 k-points to the points of a 4 x 4 x 4 grid.
All inputs are finite; a program needn't handle non-finite values.
Results may differ from the reference program's by a relative error of at most 0.0003.
Values sent between devices are 32-bit elements; how exact they have to be, the bound alone decides.
A program may use at most 128 MiB of HBM per device.

```python
import math
import jax
import jax.numpy as jnp
from jax import lax

KG = 4
K = 64
NMU = 512
C = 256
V = 256
NVEC = 2


def draw_offset_table(key, part):
    placed = jax.random.permutation(jax.random.fold_in(key, 11), K).astype(jnp.int32)
    first_axis = placed // (KG * KG)
    second_axis = placed // KG % KG
    third_axis = placed % KG
    first_diff = (first_axis[:, None] - first_axis[None, :]) % KG
    second_diff = (second_axis[:, None] - second_axis[None, :]) % KG
    third_diff = (third_axis[:, None] - third_axis[None, :]) % KG
    return (first_diff * KG * KG + second_diff * KG + third_diff).astype(jnp.int32)


def steps_of(own_key, shape, split, low, high):
    factor_of = 1.0
    for position, parts in split:
        draws = jax.random.uniform(jax.random.fold_in(jax.random.fold_in(own_key, 6), position), (parts,), jnp.float32, low / len(split), high / len(split))
        factor_of = factor_of * jnp.repeat(jnp.exp(draws), shape[position] // parts).reshape((-1,) + (1,) * (len(shape) - 1 - position))
    return factor_of


def centred(stream_key, dims, width, bound, pieces=(), kind=jnp.bfloat16):
    level = steps_of(stream_key, dims, pieces, -0.22, 0.18) if pieces else 1.0
    array = jax.random.normal(stream_key, dims, jnp.float32) * width * level
    return jnp.minimum(jnp.maximum(array, -bound), bound).astype(kind)


def setup_inputs(seed: int = 0) -> dict:
    arg_keys = jax.random.split(jax.random.key(seed), 8)
    return {
        "amplitudes": centred(arg_keys[0], (C, K, 2, NVEC, V), 1.0, 6.0, ((0, 2), (1, 16)), jnp.float32),
        "conduction_values": centred(arg_keys[1], (2, NMU, K, C), 0.0625, 0.375, ((1, 2), (2, 16)), jnp.float32),
        "valence_values": centred(arg_keys[2], (2, NMU, K, V), 0.0625, 0.375, ((1, 2), (2, 16)), jnp.float32),
        "screened": centred(arg_keys[3], (2, K, NMU, NMU), 0.004, 0.024, ((2, 16), (3, 2)), jnp.float32),
        "conduction_energy": jnp.clip(0.5 + 0.5 * jax.random.uniform(arg_keys[4], (C, K), jnp.float32) ** steps_of(arg_keys[4], (C, K), ((0, 2), (1, 16)), -0.2, 0.2), 0.5, 1.0),
        "valence_energy": jnp.clip(-0.5 + 0.5 * jax.random.uniform(arg_keys[5], (K, V), jnp.float32) ** steps_of(arg_keys[5], (K, V), ((0, 16),), -0.2, 0.2), -0.5, 0.0),
        "offset_table": draw_offset_table(jax.random.fold_in(arg_keys[7], 71), 0),
    }


def product(formula, left, right):
    return jnp.einsum(formula, left, right, precision=lax.Precision.HIGHEST)


def complex_multiply(formula, left_pair, right_pair):
    real_part = product(formula, left_pair[0], right_pair[0]) - product(formula, left_pair[1], right_pair[1])
    imag_part = product(formula, left_pair[0], right_pair[1]) + product(formula, left_pair[1], right_pair[0])
    return real_part, imag_part


def conjugated_rows(pair):
    return pair[0], -pair[1]


def decode(flat, grid_side):
    return jnp.stack([flat // (grid_side * grid_side), (flat // grid_side) % grid_side, flat % grid_side], axis=0)


def phase_table(left_flat, right_flat, grid_side):
    turns = jnp.sum(decode(left_flat, grid_side)[:, :, None] * decode(right_flat, grid_side)[:, None, :], axis=0) % grid_side
    angle = turns.astype(jnp.float32) * (2.0 * math.pi / grid_side)
    return jnp.cos(angle), -jnp.sin(angle)


def spectral(kernel_block, weight_pair, forward):
    moments = complex_multiply("rk,sknm->srnm", forward, (kernel_block[0], kernel_block[1]))
    scaled_real = weight_pair[0][None] * moments[0] - weight_pair[1][None] * moments[1]
    scaled_imag = weight_pair[0][None] * moments[1] + weight_pair[1][None] * moments[0]
    result = complex_multiply("rk,srnm->sknm", conjugated_rows(forward), (scaled_real, scaled_imag))
    return jnp.stack(result, axis=0) / forward[0].shape[0]


def reference(amplitudes, conduction_values, valence_values, screened, conduction_energy, valence_energy, offset_table):
    frequencies = jnp.arange(K, dtype=jnp.int32)
    forward = phase_table(frequencies, offset_table[:, 0].astype(jnp.int32), KG)
    forward_grid = phase_table(frequencies, frequencies, KG)
    valence_couple = (valence_values[0], valence_values[1])
    energy = (conduction_energy[:, :, None] - valence_energy[None])[:, :, None, None, :]
    kernel_block = min(NMU, 128)
    block_count = NMU // kernel_block

    def apply(state):
        state_pair = (state[:, :, 0], state[:, :, 1])

        def step(carry, block_index):
            start = (block_index * kernel_block).astype(jnp.int32)
            cond_block = tuple(lax.dynamic_slice_in_dim(part, start, kernel_block, 0) for part in (conduction_values[0], conduction_values[1]))
            weight_block = tuple(lax.dynamic_slice_in_dim(part, start, kernel_block, 2) for part in (screened[0], screened[1]))
            weights = complex_multiply("rq,qnm->rnm", forward_grid, weight_block)
            mixed_orbitals = complex_multiply("mkc,cksv->skmv", cond_block, state_pair)
            orbital_pairs = complex_multiply("zudg,cug->zucd", mixed_orbitals, conjugated_rows(valence_couple))
            convolution_result = spectral(jnp.stack(orbital_pairs, axis=0), weights, forward)
            summed_terms = complex_multiply("bxra,rxo->bxao", (convolution_result[0], convolution_result[1]), valence_couple)
            term = complex_multiply("mkc,skmv->cksv", conjugated_rows(cond_block), summed_terms)
            return (carry[0] + term[0], carry[1] + term[1]), None

        zeros = jnp.zeros(state_pair[0].shape, jnp.float32)
        total, unused = lax.scan(step, (zeros, zeros), jnp.arange(block_count, dtype=jnp.int32))
        return energy * state + jnp.stack(total, axis=2)

    first = apply(amplitudes)
    return first, apply(first)
```

```python
import functools
import math

import jax
import jax.numpy as jnp
from jax import lax
from jax.experimental import pallas as pl
from jax.experimental.pallas import tpu as pltpu
from jax.sharding import PartitionSpec as P

KG = 4
GROUPS = 2
VMEM_LIMIT = 48 * 1024 * 1024


def halves(x):
    high = x.astype(jnp.bfloat16)
    return high, (x - high.astype(jnp.float32)).astype(jnp.bfloat16)


def dot_split(left, right, dims):
    mul = functools.partial(
        lax.dot_general, dimension_numbers=(dims, ((), ())), preferred_element_type=jnp.float32
    )
    return mul(left[0], right[0]) + (mul(left[0], right[1]) + mul(left[1], right[0]))


NN = ((1,), (0,))
NT = ((1,), (1,))


def expand_kernel(b_ref, p_ref, q_ref, m_ref, x_high, x_low):
    @pl.when(pl.program_id(1) == 0)
    def _():
        br, bi = b_ref[0, 0], b_ref[0, 1]
        wide = jnp.concatenate(
            [jnp.concatenate([br, bi], axis=1), jnp.concatenate([-bi, br], axis=1)], axis=0
        )
        orbitals = jnp.concatenate([p_ref[0, 0], p_ref[0, 1]], axis=1)
        x = dot_split(halves(orbitals), halves(wide), NN)
        high, low = halves(x)
        x_high[...] = high
        x_low[...] = low

    qr, qi = q_ref[0, 0], q_ref[0, 1]
    rows = jnp.concatenate(
        [jnp.concatenate([qr, qi], axis=1), jnp.concatenate([-qi, qr], axis=1)], axis=0
    )
    m = dot_split(halves(rows), (x_high[...], x_low[...]), NT)
    count = qr.shape[0]
    owners, _, _, second, first = m_ref.shape
    m_ref[:, 0, 0] = m[:count].reshape(owners, second, first)
    m_ref[:, 0, 1] = m[count:].reshape(owners, second, first)


def expand_pairs(b, p, q, owners, tiles):
    kc, _, cond, val = b.shape
    points = p.shape[2]
    per = points // tiles
    second = points // owners
    return pl.pallas_call(
        expand_kernel,
        grid=(kc, tiles),
        in_specs=[
            pl.BlockSpec((1, 2, cond, val), lambda k, t: (k, 0, 0, 0)),
            pl.BlockSpec((1, 2, points, cond), lambda k, t: (k, 0, 0, 0)),
            pl.BlockSpec((1, 2, per, val), lambda k, t: (k, 0, t, 0)),
        ],
        out_specs=pl.BlockSpec(
            (owners // tiles, 1, 2, second, points), lambda k, t: (t, k, 0, 0, 0)
        ),
        out_shape=jax.ShapeDtypeStruct((owners, kc, 2, second, points), jnp.float32),
        scratch_shapes=[pltpu.VMEM((points, 2 * val), jnp.bfloat16)] * 2,
        compiler_params=pltpu.CompilerParams(vmem_limit_bytes=VMEM_LIMIT),
        cost_estimate=pl.CostEstimate(
            flops=kc * 24 * points * val * (cond + points),
            bytes_accessed=kc * 8 * (cond * val + points * (cond + val + points)),
            transcendentals=0,
        ),
        name="expand",
    )(b, p, q)


def contract_kernel(n_ref, qt_ref, pt_ref, b_ref, ec_ref, ev_ref, out_ref, z_ref):
    owners, _, _, second, first = n_ref.shape
    nr = n_ref[:, 0, 0].reshape(owners * second, first)
    ni = n_ref[:, 0, 1].reshape(owners * second, first)
    pairs = jnp.concatenate([nr, ni], axis=0)
    qr, qi = qt_ref[0, 0], qt_ref[0, 1]
    rows = jnp.concatenate(
        [jnp.concatenate([qr, -qi], axis=1), jnp.concatenate([qi, qr], axis=1)], axis=0
    )
    part = dot_split(halves(rows), halves(pairs), NN)

    @pl.when(pl.program_id(1) == 0)
    def _():
        z_ref[...] = part

    @pl.when(pl.program_id(1) > 0)
    def _():
        z_ref[...] += part

    @pl.when(pl.program_id(1) == pl.num_programs(1) - 1)
    def _():
        val = qr.shape[0]
        z = jnp.concatenate([z_ref[:val], z_ref[val:]], axis=1)
        pr, pi = pt_ref[0, 0], pt_ref[0, 1]
        cond = pr.shape[0]
        left = jnp.concatenate(
            [jnp.concatenate([pr, pi], axis=1), jnp.concatenate([-pi, pr], axis=1)], axis=0
        )
        y = dot_split(halves(left), halves(z), NT)
        energy = ec_ref[0] - ev_ref[0]
        out_ref[0, 0] = energy * b_ref[0, 0] + y[:cond]
        out_ref[0, 1] = energy * b_ref[0, 1] + y[cond:]


def contract_pairs(n, qt, pt, b, ec, ev, tiles):
    kc, _, cond, val = b.shape
    owners, _, _, second, points = n.shape
    per = points // tiles
    return pl.pallas_call(
        contract_kernel,
        grid=(kc, tiles),
        in_specs=[
            pl.BlockSpec((owners // tiles, 1, 2, second, points), lambda k, t: (t, k, 0, 0, 0)),
            pl.BlockSpec((1, 2, val, per), lambda k, t: (k, 0, 0, t)),
            pl.BlockSpec((1, 2, cond, points), lambda k, t: (k, 0, 0, 0)),
            pl.BlockSpec((1, 2, cond, val), lambda k, t: (k, 0, 0, 0)),
            pl.BlockSpec((1, cond, 1), lambda k, t: (k, 0, 0)),
            pl.BlockSpec((1, 1, val), lambda k, t: (k, 0, 0)),
        ],
        out_specs=pl.BlockSpec((1, 2, cond, val), lambda k, t: (k, 0, 0, 0)),
        out_shape=jax.ShapeDtypeStruct((kc, 2, cond, val), jnp.float32),
        scratch_shapes=[pltpu.VMEM((2 * val, points), jnp.float32)],
        compiler_params=pltpu.CompilerParams(vmem_limit_bytes=VMEM_LIMIT),
        cost_estimate=pl.CostEstimate(
            flops=kc * 24 * points * val * (cond + points),
            bytes_accessed=kc * 8 * (2 * cond * val + points * (cond + val + points)),
            transcendentals=0,
        ),
        name="contract",
    )(n, qt, pt, b, ec, ev)


def dft4(points, inverse):
    (ar, ai), (br, bi), (cr, ci), (dr, di) = points
    sr, si, tr, ti = ar + cr, ai + ci, ar - cr, ai - ci
    ur, ui, wr, wi = br + dr, bi + di, br - dr, bi - di
    minus = (tr + wi, ti - wr)
    plus = (tr - wi, ti + wr)
    one, three = (plus, minus) if inverse else (minus, plus)
    return [(sr + ur, si + ui), one, (sr - ur, si - ui), three]


def dft16(values, inverse):
    side = KG
    for start, stride in ((1, side), (side, 1)):
        for line in range(side):
            places = [line * stride + step * start for step in range(side)]
            for place, value in zip(places, dft4([values[q] for q in places], inverse)):
                values[place] = value
    return values


def planes(load, store, lanes, inverse):
    side = KG
    plane = side * side

    def body(index, carry):
        base = index * plane
        for lane in range(lanes):
            values = [load(base + j, lane) for j in range(plane)]
            for j, value in enumerate(dft16(values, inverse)):
                store(base + j, lane, value)
        return carry

    lax.fori_loop(0, side, body, 0)


def weight_kernel(w_ref, out_ref):
    side = KG
    plane = side * side
    lanes = w_ref.shape[3] // 128
    scale = 1.0 / (plane * side)

    def at(lane):
        return pl.ds(lane * 128, 128)

    def load(f, lane):
        return (w_ref[0, f, :, at(lane)], w_ref[1, f, :, at(lane)])

    def store(f, lane, value):
        out_ref[f, 0, :, at(lane)] = value[0]
        out_ref[f, 1, :, at(lane)] = value[1]

    planes(load, store, lanes, False)

    def body(j, carry):
        for lane in range(lanes):
            spots = [j + plane * a for a in range(side)]
            values = [(out_ref[f, 0, :, at(lane)], out_ref[f, 1, :, at(lane)]) for f in spots]
            for f, value in zip(spots, dft4(values, False)):
                store(f, lane, (value[0] * scale, value[1] * scale))
        return carry

    lax.fori_loop(0, plane, body, 0)


def weight_transform(screened):
    _, count, second, first = screened.shape
    return pl.pallas_call(
        weight_kernel,
        grid=(second // 8,),
        in_specs=[pl.BlockSpec((2, count, 8, first), lambda i: (0, 0, i, 0))],
        out_specs=pl.BlockSpec((count, 2, 8, first), lambda i: (0, 0, i, 0)),
        out_shape=jax.ShapeDtypeStruct((count, 2, second, first), jnp.float32),
        compiler_params=pltpu.CompilerParams(vmem_limit_bytes=VMEM_LIMIT),
        cost_estimate=pl.CostEstimate(
            flops=30 * screened.size, bytes_accessed=8 * screened.size, transcendentals=0
        ),
        name="weight_transform",
    )(screened)


def spectral_kernel(groups, place_ref, *refs):
    m_refs, w_ref, n_refs, s_ref = refs[:groups], refs[groups], refs[groups + 1 : -1], refs[-1]
    side = KG
    plane = side * side
    lanes = s_ref.shape[3] // 128
    owners, kc = m_refs[0].shape[:2]

    def at(lane):
        return pl.ds(lane * 128, 128)

    def load(f, lane):
        return (s_ref[f, 0, :, at(lane)], s_ref[f, 1, :, at(lane)])

    def store(f, lane, value):
        s_ref[f, 0, :, at(lane)] = value[0]
        s_ref[f, 1, :, at(lane)] = value[1]

    def scatter(owner, carry):
        for g in range(groups):
            for k in range(kc):
                s_ref[place_ref[(owner * groups + g) * kc + k]] = m_refs[g][owner, k]
        return carry

    def gather(owner, carry):
        for g in range(groups):
            for k in range(kc):
                n_refs[g][owner, k] = s_ref[place_ref[(owner * groups + g) * kc + k]]
        return carry

    def middle(j, carry):
        for lane in range(lanes):
            spots = [j + plane * a for a in range(side)]
            scaled = []
            for f, (vr, vi) in zip(spots, dft4([load(f, lane) for f in spots], False)):
                wr, wi = w_ref[0, f, 0, :, at(lane)], w_ref[0, f, 1, :, at(lane)]
                scaled.append((wr * vr - wi * vi, wr * vi + wi * vr))
            for f, value in zip(spots, dft4(scaled, True)):
                store(f, lane, value)
        return carry

    lax.fori_loop(0, owners, scatter, 0)
    planes(load, store, lanes, False)
    lax.fori_loop(0, plane, middle, 0)
    planes(load, store, lanes, True)
    lax.fori_loop(0, owners, gather, 0)


def spectral_grid(place, blocks, weights):
    groups = len(blocks)
    owners, kc, _, second, points = blocks[0].shape
    parts, count, _, _, first = weights.shape
    spec = pl.BlockSpec((owners, kc, 2, 8, first), lambda h, i, place: (0, 0, 0, i, h))
    shape = jax.ShapeDtypeStruct(blocks[0].shape, jnp.float32)
    return pl.pallas_call(
        functools.partial(spectral_kernel, groups),
        grid_spec=pltpu.PrefetchScalarGridSpec(
            num_scalar_prefetch=1,
            grid=(parts, second // 8),
            in_specs=[spec] * groups
            + [pl.BlockSpec((1, count, 2, 8, first), lambda h, i, place: (h, 0, 0, i, 0))],
            out_specs=[spec] * groups,
            scratch_shapes=[pltpu.VMEM((count, 2, 8, first), jnp.float32)],
        ),
        out_shape=[shape] * groups,
        compiler_params=pltpu.CompilerParams(vmem_limit_bytes=VMEM_LIMIT),
        cost_estimate=pl.CostEstimate(
            flops=60 * groups * blocks[0].size,
            bytes_accessed=12 * groups * blocks[0].size,
            transcendentals=0,
        ),
        name="spectral",
    )(place, *blocks, weights)


def by_vector(
    amplitudes,
    conduction_values,
    valence_values,
    screened,
    conduction_energy,
    valence_energy,
    offset_table,
):
    owners = lax.axis_size("ka")
    local_kpts = amplitudes.shape[1]
    groups = math.gcd(GROUPS, local_kpts)
    kc = local_kpts // groups
    tiles = math.gcd(4, owners)
    me = lax.axis_index("rows")
    swap = [(0, 1), (1, 0)]
    place = offset_table[:, 0]
    spans = [slice(g * kc, (g + 1) * kc) for g in range(groups)]

    def ordered(own, other, axis):
        lower = me == 0
        return jnp.concatenate(
            [jnp.where(lower, own, other), jnp.where(lower, other, own)], axis=axis
        )

    def vector(block, index):
        picked = lax.dynamic_index_in_dim(block, index, 3, keepdims=False)
        return picked.transpose(1, 2, 0, 3)

    states, conds, vals, conds_t, vals_t, ecs, evs = [], [], [], [], [], [], []
    for span in spans:
        block = amplitudes[:, span]
        other = lax.ppermute(vector(block, 1 - me), "rows", swap)
        states.append(ordered(vector(block, me), other, 2))
        cond = conduction_values[:, :, span].transpose(2, 0, 1, 3)
        conds.append(lax.all_gather(cond, "rows", axis=2, tiled=True))
        val = valence_values[:, :, span].transpose(2, 0, 1, 3)
        vals.append(lax.all_gather(val, "rows", axis=2, tiled=True))
        conds_t.append(conds[-1].transpose(0, 1, 3, 2))
        vals_t.append(vals[-1].transpose(0, 1, 3, 2))
        ecs.append(conduction_energy[:, span].T[:, :, None])
        evs.append(valence_energy[span][:, None, :])
    ecs = [lax.all_gather(ec, "rows", axis=1, tiled=True) for ec in ecs]
    weights = lax.all_gather(weight_transform(screened), "rows", axis=0)

    def apply(states):
        sent = [
            lax.all_to_all(expand_pairs(b, p, q, owners, tiles), "ka", 0, 0, tiled=True)
            for b, p, q in zip(states, conds, vals)
        ]
        back = [
            lax.all_to_all(n, "ka", 0, 0, tiled=True) for n in spectral_grid(place, sent, weights)
        ]
        return [
            contract_pairs(*args, tiles) for args in zip(back, vals_t, conds_t, states, ecs, evs)
        ]

    def finish(states):
        results = []
        for state in states:
            rows = state.shape[2] // 2
            mine = lax.dynamic_slice_in_dim(state, me * rows, rows, 2)
            theirs = lax.dynamic_slice_in_dim(state, (1 - me) * rows, rows, 2)
            other = lax.ppermute(theirs, "rows", swap)
            both = jnp.stack(
                [jnp.where(me == 0, mine, other), jnp.where(me == 0, other, mine)], axis=3
            )
            results.append(both.transpose(2, 0, 1, 3, 4))
        return jnp.concatenate(results, axis=1)

    first = apply(states)
    return finish(first), finish(apply(first))


def product(formula, left, right):
    return jnp.einsum(formula, left, right, precision=lax.Precision.HIGHEST)


def complex_multiply(formula, left_pair, right_pair):
    real_part = product(formula, left_pair[0], right_pair[0]) - product(
        formula, left_pair[1], right_pair[1]
    )
    imag_part = product(formula, left_pair[0], right_pair[1]) + product(
        formula, left_pair[1], right_pair[0]
    )
    return (real_part, imag_part)


def conjugated_rows(pair):
    return (pair[0], -pair[1])


def decode(flat, grid_side):
    return jnp.stack(
        [flat // (grid_side * grid_side), flat // grid_side % grid_side, flat % grid_side], axis=0
    )


def phase_table(left_flat, right_flat, grid_side):
    turns = (
        jnp.sum(
            decode(left_flat, grid_side)[:, :, None] * decode(right_flat, grid_side)[:, None, :],
            axis=0,
        )
        % grid_side
    )
    angle = turns.astype(jnp.float32) * (2.0 * math.pi / grid_side)
    return (jnp.cos(angle), -jnp.sin(angle))


def spectral(kernel_block, weight_pair, forward):
    moments = complex_multiply("rk,sknm->srnm", forward, (kernel_block[0], kernel_block[1]))
    scaled_real = weight_pair[0][None] * moments[0] - weight_pair[1][None] * moments[1]
    scaled_imag = weight_pair[0][None] * moments[1] + weight_pair[1][None] * moments[0]
    result = complex_multiply("rk,srnm->sknm", conjugated_rows(forward), (scaled_real, scaled_imag))
    return jnp.stack(result, axis=0) / forward[0].shape[0]


def expand(mixed_component, valence_component):
    orbital_pairs = complex_multiply(
        "zudg,cug->zucd", mixed_component, conjugated_rows(valence_component)
    )
    return jnp.stack(orbital_pairs, axis=0)


def contract(kernel_block, valence_component):
    return complex_multiply("bxra,rxo->bxao", (kernel_block[0], kernel_block[1]), valence_component)


def per_device(
    amplitudes,
    conduction_values,
    valence_values,
    screened,
    conduction_energy,
    valence_energy,
    offset_table,
):
    ka_count = lax.axis_size("ka")
    points_all = lax.all_gather(valence_values, "rows", axis=1, tiled=True)
    valence_couple = (points_all[0], points_all[1])
    cond_pair = (conduction_values[0], conduction_values[1])
    frequencies = jnp.arange(offset_table.shape[0], dtype=jnp.int32)
    forward = phase_table(frequencies, offset_table[:, 0], KG)
    forward_grid = phase_table(frequencies, frequencies, KG)
    weights = complex_multiply("rq,qnm->rnm", forward_grid, (screened[0], screened[1]))
    energy = (conduction_energy[:, :, None] - valence_energy[None])[:, :, None, None, :]
    local_second = screened.shape[2]
    half_second = local_second // 2
    local_kpts = valence_values.shape[2]
    band_count = valence_values.shape[3]

    def apply(state):
        whole = lax.all_gather(state, "rows", axis=0, tiled=True)
        mixed_orbitals = complex_multiply(
            "mkc,cksv->skmv", cond_pair, (whole[:, :, 0], whole[:, :, 1])
        )
        partials = []
        for piece_index in range(2):
            sub_valence = tuple(
                (
                    part.reshape(ka_count, 2, half_second, local_kpts, band_count)[
                        :, piece_index
                    ].reshape(ka_count * half_second, local_kpts, band_count)
                    for part in valence_couple
                )
            )
            sub_weights = tuple(
                (
                    part[:, piece_index * half_second : (piece_index + 1) * half_second]
                    for part in weights
                )
            )
            sent = lax.all_to_all(
                expand(mixed_orbitals, sub_valence), "ka", split_axis=3, concat_axis=2, tiled=True
            )
            back = lax.all_to_all(
                spectral(sent, sub_weights, forward), "ka", split_axis=2, concat_axis=3, tiled=True
            )
            partials.append(contract(back, sub_valence))
        summed_terms = (partials[0][0] + partials[1][0], partials[0][1] + partials[1][1])
        sliced = tuple((part for part in cond_pair))
        result = complex_multiply("mkc,skmv->cksv", conjugated_rows(sliced), summed_terms)
        kernel = lax.psum_scatter(
            jnp.stack(result, axis=2), "rows", scatter_dimension=0, tiled=True
        )
        return energy * state + kernel

    first = apply(amplitudes)
    return (first, apply(first))


def solution(mesh):
    placed = (
        P("rows", "ka", None, None, None),
        P(None, "rows", "ka", None),
        P(None, "rows", "ka", None),
        P(None, None, "ka", "rows"),
        P("rows", "ka"),
        P("ka", None),
        P(),
    )

    def run(*arrays):
        vectors, rows = arrays[0].shape[3], mesh.shape["rows"]
        return spread(by_vector if vectors == rows == 2 else per_device)(*arrays)

    spread = lambda part: jax.shard_map(
        part,
        mesh=mesh,
        in_specs=placed,
        out_specs=(P("rows", "ka", None, None, None), P("rows", "ka", None, None, None)),
        check_vma=False,
    )
    return run
```

```python
import functools
import math

import jax
import jax.numpy as jnp
from jax import lax
from jax.experimental import pallas as pl
from jax.experimental.pallas import tpu as pltpu
from jax.sharding import PartitionSpec as P

KG = 4
VMEM_LIMIT = 48 * 1024 * 1024


def halves(x):
    high = x.astype(jnp.bfloat16)
    return high, (x - high.astype(jnp.float32)).astype(jnp.bfloat16)


def dot_split(left, right, dims):
    mul = functools.partial(
        lax.dot_general, dimension_numbers=(dims, ((), ())), preferred_element_type=jnp.float32
    )
    return mul(left[0], right[0]) + (mul(left[0], right[1]) + mul(left[1], right[0]))


NN = ((1,), (0,))
NT = ((1,), (1,))


def expand_kernel(b_ref, p_ref, q_ref, m_ref, x_high, x_low):
    @pl.when(pl.program_id(1) == 0)
    def _():
        br, bi = b_ref[0, 0], b_ref[0, 1]
        wide = jnp.concatenate(
            [jnp.concatenate([br, bi], axis=1), jnp.concatenate([-bi, br], axis=1)], axis=0
        )
        orbitals = jnp.concatenate([p_ref[0, 0], p_ref[0, 1]], axis=1)
        x = dot_split(halves(orbitals), halves(wide), NN)
        high, low = halves(x)
        x_high[...] = high
        x_low[...] = low

    qr, qi = q_ref[0, 0], q_ref[0, 1]
    rows = jnp.concatenate(
        [jnp.concatenate([qr, qi], axis=1), jnp.concatenate([-qi, qr], axis=1)], axis=0
    )
    m = dot_split(halves(rows), (x_high[...], x_low[...]), NT)
    count = qr.shape[0]
    owners, _, _, second, first = m_ref.shape
    m_ref[:, 0, 0] = m[:count].reshape(owners, second, first)
    m_ref[:, 0, 1] = m[count:].reshape(owners, second, first)


def expand_pairs(b, p, q, owners, tiles):
    kc, _, cond, val = b.shape
    points = p.shape[2]
    per = points // tiles
    second = points // owners
    return pl.pallas_call(
        expand_kernel,
        grid=(kc, tiles),
        in_specs=[
            pl.BlockSpec((1, 2, cond, val), lambda k, t: (k, 0, 0, 0)),
            pl.BlockSpec((1, 2, points, cond), lambda k, t: (k, 0, 0, 0)),
            pl.BlockSpec((1, 2, per, val), lambda k, t: (k, 0, t, 0)),
        ],
        out_specs=pl.BlockSpec(
            (owners // tiles, 1, 2, second, points), lambda k, t: (t, k, 0, 0, 0)
        ),
        out_shape=jax.ShapeDtypeStruct((owners, kc, 2, second, points), jnp.float32),
        scratch_shapes=[pltpu.VMEM((points, 2 * val), jnp.bfloat16)] * 2,
        compiler_params=pltpu.CompilerParams(vmem_limit_bytes=VMEM_LIMIT),
        cost_estimate=pl.CostEstimate(
            flops=kc * 24 * points * val * (cond + points),
            bytes_accessed=kc * 8 * (cond * val + points * (cond + val + points)),
            transcendentals=0,
        ),
        name="expand",
    )(b, p, q)


def contract_kernel(n_ref, qt_ref, pt_ref, b_ref, ec_ref, ev_ref, out_ref, z_ref):
    owners, _, _, second, first = n_ref.shape
    nr = n_ref[:, 0, 0].reshape(owners * second, first)
    ni = n_ref[:, 0, 1].reshape(owners * second, first)
    pairs = jnp.concatenate([nr, ni], axis=0)
    qr, qi = qt_ref[0, 0], qt_ref[0, 1]
    rows = jnp.concatenate(
        [jnp.concatenate([qr, -qi], axis=1), jnp.concatenate([qi, qr], axis=1)], axis=0
    )
    part = dot_split(halves(rows), halves(pairs), NN)

    @pl.when(pl.program_id(1) == 0)
    def _():
        z_ref[...] = part

    @pl.when(pl.program_id(1) > 0)
    def _():
        z_ref[...] += part

    @pl.when(pl.program_id(1) == pl.num_programs(1) - 1)
    def _():
        val = qr.shape[0]
        z = jnp.concatenate([z_ref[:val], z_ref[val:]], axis=1)
        pr, pi = pt_ref[0, 0], pt_ref[0, 1]
        cond = pr.shape[0]
        left = jnp.concatenate(
            [jnp.concatenate([pr, pi], axis=1), jnp.concatenate([-pi, pr], axis=1)], axis=0
        )
        y = dot_split(halves(left), halves(z), NT)
        energy = ec_ref[0] - ev_ref[0]
        out_ref[0, 0] = energy * b_ref[0, 0] + y[:cond]
        out_ref[0, 1] = energy * b_ref[0, 1] + y[cond:]


def contract_pairs(n, qt, pt, b, ec, ev, tiles):
    kc, _, cond, val = b.shape
    owners, _, _, second, points = n.shape
    per = points // tiles
    return pl.pallas_call(
        contract_kernel,
        grid=(kc, tiles),
        in_specs=[
            pl.BlockSpec((owners // tiles, 1, 2, second, points), lambda k, t: (t, k, 0, 0, 0)),
            pl.BlockSpec((1, 2, val, per), lambda k, t: (k, 0, 0, t)),
            pl.BlockSpec((1, 2, cond, points), lambda k, t: (k, 0, 0, 0)),
            pl.BlockSpec((1, 2, cond, val), lambda k, t: (k, 0, 0, 0)),
            pl.BlockSpec((1, cond, 1), lambda k, t: (k, 0, 0)),
            pl.BlockSpec((1, 1, val), lambda k, t: (k, 0, 0)),
        ],
        out_specs=pl.BlockSpec((1, 2, cond, val), lambda k, t: (k, 0, 0, 0)),
        out_shape=jax.ShapeDtypeStruct((kc, 2, cond, val), jnp.float32),
        scratch_shapes=[pltpu.VMEM((2 * val, points), jnp.float32)],
        compiler_params=pltpu.CompilerParams(vmem_limit_bytes=VMEM_LIMIT),
        cost_estimate=pl.CostEstimate(
            flops=kc * 24 * points * val * (cond + points),
            bytes_accessed=kc * 8 * (2 * cond * val + points * (cond + val + points)),
            transcendentals=0,
        ),
        name="contract",
    )(n, qt, pt, b, ec, ev)


def dft4(points, inverse):
    (ar, ai), (br, bi), (cr, ci), (dr, di) = points
    sr, si, tr, ti = ar + cr, ai + ci, ar - cr, ai - ci
    ur, ui, wr, wi = br + dr, bi + di, br - dr, bi - di
    minus = (tr + wi, ti - wr)
    plus = (tr - wi, ti + wr)
    one, three = (plus, minus) if inverse else (minus, plus)
    return [(sr + ur, si + ui), one, (sr - ur, si - ui), three]


def dft16(values, inverse):
    side = KG
    for start, stride in ((1, side), (side, 1)):
        for line in range(side):
            places = [line * stride + step * start for step in range(side)]
            for place, value in zip(places, dft4([values[q] for q in places], inverse)):
                values[place] = value
    return values


def planes(load, store, lanes, inverse):
    side = KG
    plane = side * side

    def body(index, carry):
        base = index * plane
        for lane in range(lanes):
            values = [load(base + j, lane) for j in range(plane)]
            for j, value in enumerate(dft16(values, inverse)):
                store(base + j, lane, value)
        return carry

    lax.fori_loop(0, side, body, 0)


def weight_kernel(w_ref, out_ref):
    side = KG
    plane = side * side
    lanes = w_ref.shape[3] // 128
    scale = 1.0 / (plane * side)

    def at(lane):
        return pl.ds(lane * 128, 128)

    def load(f, lane):
        return (w_ref[0, f, :, at(lane)], w_ref[1, f, :, at(lane)])

    def store(f, lane, value):
        out_ref[f, 0, :, at(lane)] = value[0]
        out_ref[f, 1, :, at(lane)] = value[1]

    planes(load, store, lanes, False)

    def body(j, carry):
        for lane in range(lanes):
            spots = [j + plane * a for a in range(side)]
            values = [(out_ref[f, 0, :, at(lane)], out_ref[f, 1, :, at(lane)]) for f in spots]
            for f, value in zip(spots, dft4(values, False)):
                store(f, lane, (value[0] * scale, value[1] * scale))
        return carry

    lax.fori_loop(0, plane, body, 0)


def weight_transform(screened):
    _, count, second, first = screened.shape
    return pl.pallas_call(
        weight_kernel,
        grid=(second // 8,),
        in_specs=[pl.BlockSpec((2, count, 8, first), lambda i: (0, 0, i, 0))],
        out_specs=pl.BlockSpec((count, 2, 8, first), lambda i: (0, 0, i, 0)),
        out_shape=jax.ShapeDtypeStruct((count, 2, second, first), jnp.float32),
        compiler_params=pltpu.CompilerParams(vmem_limit_bytes=VMEM_LIMIT),
        cost_estimate=pl.CostEstimate(
            flops=30 * screened.size, bytes_accessed=8 * screened.size, transcendentals=0
        ),
        name="weight_transform",
    )(screened)


def spectral_kernel(into, outof, place_ref, *refs):
    m_refs, w_ref = refs[: len(into)], refs[len(into)]
    n_refs, s_ref = refs[len(into) + 1 : -1], refs[-1]
    side = KG
    plane = side * side
    lanes = s_ref.shape[3] // 128
    owners = m_refs[0].shape[0]
    kpts = s_ref.shape[0] // owners

    def at(lane):
        return pl.ds(lane * 128, 128)

    def load(f, lane):
        return (s_ref[f, 0, :, at(lane)], s_ref[f, 1, :, at(lane)])

    def store(f, lane, value):
        s_ref[f, 0, :, at(lane)] = value[0]
        s_ref[f, 1, :, at(lane)] = value[1]

    def scatter(owner, carry):
        for ref, (start, count) in zip(m_refs, into):
            for k in range(count):
                s_ref[place_ref[owner * kpts + start + k]] = ref[owner, k]
        return carry

    def gather(owner, carry):
        for ref, (start, count) in zip(n_refs, outof):
            for k in range(count):
                ref[owner, k] = s_ref[place_ref[owner * kpts + start + k]]
        return carry

    def middle(j, carry):
        for lane in range(lanes):
            spots = [j + plane * a for a in range(side)]
            scaled = []
            for f, (vr, vi) in zip(spots, dft4([load(f, lane) for f in spots], False)):
                wr, wi = w_ref[0, f, 0, :, at(lane)], w_ref[0, f, 1, :, at(lane)]
                scaled.append((wr * vr - wi * vi, wr * vi + wi * vr))
            for f, value in zip(spots, dft4(scaled, True)):
                store(f, lane, value)
        return carry

    lax.fori_loop(0, owners, scatter, 0)
    planes(load, store, lanes, False)
    lax.fori_loop(0, plane, middle, 0)
    planes(load, store, lanes, True)
    lax.fori_loop(0, owners, gather, 0)


def spectral_grid(place, blocks, weights, into, outof):
    owners, _, _, second, points = blocks[0].shape
    parts, count, _, _, first = weights.shape
    size = 2 * count * second * points

    def spec(kc):
        return pl.BlockSpec((owners, kc, 2, 8, first), lambda h, i, place: (0, 0, 0, i, h))

    return pl.pallas_call(
        functools.partial(spectral_kernel, into, outof),
        grid_spec=pltpu.PrefetchScalarGridSpec(
            num_scalar_prefetch=1,
            grid=(parts, second // 8),
            in_specs=[spec(kc) for _, kc in into]
            + [pl.BlockSpec((1, count, 2, 8, first), lambda h, i, place: (h, 0, 0, i, 0))],
            out_specs=[spec(kc) for _, kc in outof],
            scratch_shapes=[pltpu.VMEM((count, 2, 8, first), jnp.float32)],
        ),
        out_shape=[
            jax.ShapeDtypeStruct((owners, kc, 2, second, points), jnp.float32) for _, kc in outof
        ],
        compiler_params=pltpu.CompilerParams(vmem_limit_bytes=VMEM_LIMIT),
        cost_estimate=pl.CostEstimate(
            flops=60 * size, bytes_accessed=12 * size, transcendentals=0
        ),
        name="spectral",
    )(place, *blocks, weights)


def by_vector(
    amplitudes,
    conduction_values,
    valence_values,
    screened,
    conduction_energy,
    valence_energy,
    offset_table,
):
    owners = lax.axis_size("ka")
    local_kpts = amplitudes.shape[1]
    tiles = math.gcd(4, owners)
    me = lax.axis_index("rows")
    swap = [(0, 1), (1, 0)]
    place = offset_table[:, 0]
    half = max(local_kpts // 2, 1)
    usual = [(k, min(half, local_kpts - k)) for k in range(0, local_kpts, half)]

    def ordered(own, other, axis):
        lower = me == 0
        return jnp.concatenate(
            [jnp.where(lower, own, other), jnp.where(lower, other, own)], axis=axis
        )

    def vector(block, index):
        picked = lax.dynamic_index_in_dim(block, index, 3, keepdims=False)
        return picked.transpose(1, 2, 0, 3)

    def exchange(sent, after):
        if after:
            marks = [x[(0,) * x.ndim] for x in after]
            sent, _ = lax.optimization_barrier((sent, marks))
        return [lax.ppermute(x, "rows", swap) for x in sent]

    own_weights = weight_transform(screened)
    states, conds, vals, came = [], [], [], []
    for start, count in usual:
        span = slice(start, start + count)
        block = amplitudes[:, span]
        cond = conduction_values[:, :, span].transpose(2, 0, 1, 3)
        val = valence_values[:, :, span].transpose(2, 0, 1, 3)
        if came:
            cond, own_weights = lax.optimization_barrier((cond, own_weights))
        came = exchange([vector(block, 1 - me), cond, val], came)
        states.append(ordered(vector(block, me), came[0], 2))
        conds.append(ordered(cond, came[1], 2))
        vals.append(ordered(val, came[2], 2))
    weights = ordered(own_weights[None], exchange([own_weights], came)[0][None], 0)

    def send(states, conds, vals):
        return [
            lax.all_to_all(expand_pairs(b, p, q, owners, tiles), "ka", 0, 0, tiled=True)
            for b, p, q in zip(states, conds, vals)
        ]

    sent = send(states, conds, vals)
    conds_t = [x.transpose(0, 1, 3, 2) for x in conds]
    vals_t = [x.transpose(0, 1, 3, 2) for x in vals]
    all_ec = lax.all_gather(conduction_energy, "rows", axis=0, tiled=True).T[:, :, None]
    ecs = [all_ec[start : start + count] for start, count in usual]
    evs = [valence_energy[start : start + count][:, None, :] for start, count in usual]

    def receive(states, sent):
        back = [
            lax.all_to_all(n, "ka", 0, 0, tiled=True)
            for n in spectral_grid(place, sent, weights, usual, usual)
        ]
        return [
            contract_pairs(*args, tiles) for args in zip(back, vals_t, conds_t, states, ecs, evs)
        ]

    def finish(states):
        results = []
        for state in states:
            rows = state.shape[2] // 2
            mine = lax.dynamic_slice_in_dim(state, me * rows, rows, 2)
            theirs = lax.dynamic_slice_in_dim(state, (1 - me) * rows, rows, 2)
            other = lax.ppermute(theirs, "rows", swap)
            both = jnp.stack(
                [jnp.where(me == 0, mine, other), jnp.where(me == 0, other, mine)], axis=3
            )
            results.append(both.transpose(2, 0, 1, 3, 4))
        return jnp.concatenate(results, axis=1)

    first = receive(states, sent)
    second = receive(first, send(first, conds, vals))
    return finish(first), finish(second)


def product(formula, left, right):
    return jnp.einsum(formula, left, right, precision=lax.Precision.HIGHEST)


def complex_multiply(formula, left_pair, right_pair):
    real_part = product(formula, left_pair[0], right_pair[0]) - product(
        formula, left_pair[1], right_pair[1]
    )
    imag_part = product(formula, left_pair[0], right_pair[1]) + product(
        formula, left_pair[1], right_pair[0]
    )
    return (real_part, imag_part)


def conjugated_rows(pair):
    return (pair[0], -pair[1])


def decode(flat, grid_side):
    return jnp.stack(
        [flat // (grid_side * grid_side), flat // grid_side % grid_side, flat % grid_side], axis=0
    )


def phase_table(left_flat, right_flat, grid_side):
    turns = (
        jnp.sum(
            decode(left_flat, grid_side)[:, :, None] * decode(right_flat, grid_side)[:, None, :],
            axis=0,
        )
        % grid_side
    )
    angle = turns.astype(jnp.float32) * (2.0 * math.pi / grid_side)
    return (jnp.cos(angle), -jnp.sin(angle))


def spectral(kernel_block, weight_pair, forward):
    moments = complex_multiply("rk,sknm->srnm", forward, (kernel_block[0], kernel_block[1]))
    scaled_real = weight_pair[0][None] * moments[0] - weight_pair[1][None] * moments[1]
    scaled_imag = weight_pair[0][None] * moments[1] + weight_pair[1][None] * moments[0]
    result = complex_multiply("rk,srnm->sknm", conjugated_rows(forward), (scaled_real, scaled_imag))
    return jnp.stack(result, axis=0) / forward[0].shape[0]


def expand(mixed_component, valence_component):
    orbital_pairs = complex_multiply(
        "zudg,cug->zucd", mixed_component, conjugated_rows(valence_component)
    )
    return jnp.stack(orbital_pairs, axis=0)


def contract(kernel_block, valence_component):
    return complex_multiply("bxra,rxo->bxao", (kernel_block[0], kernel_block[1]), valence_component)


def per_device(
    amplitudes,
    conduction_values,
    valence_values,
    screened,
    conduction_energy,
    valence_energy,
    offset_table,
):
    ka_count = lax.axis_size("ka")
    points_all = lax.all_gather(valence_values, "rows", axis=1, tiled=True)
    valence_couple = (points_all[0], points_all[1])
    cond_pair = (conduction_values[0], conduction_values[1])
    frequencies = jnp.arange(offset_table.shape[0], dtype=jnp.int32)
    forward = phase_table(frequencies, offset_table[:, 0], KG)
    forward_grid = phase_table(frequencies, frequencies, KG)
    weights = complex_multiply("rq,qnm->rnm", forward_grid, (screened[0], screened[1]))
    energy = (conduction_energy[:, :, None] - valence_energy[None])[:, :, None, None, :]
    local_second = screened.shape[2]
    half_second = local_second // 2
    local_kpts = valence_values.shape[2]
    band_count = valence_values.shape[3]

    def apply(state):
        whole = lax.all_gather(state, "rows", axis=0, tiled=True)
        mixed_orbitals = complex_multiply(
            "mkc,cksv->skmv", cond_pair, (whole[:, :, 0], whole[:, :, 1])
        )
        partials = []
        for piece_index in range(2):
            sub_valence = tuple(
                (
                    part.reshape(ka_count, 2, half_second, local_kpts, band_count)[
                        :, piece_index
                    ].reshape(ka_count * half_second, local_kpts, band_count)
                    for part in valence_couple
                )
            )
            sub_weights = tuple(
                (
                    part[:, piece_index * half_second : (piece_index + 1) * half_second]
                    for part in weights
                )
            )
            sent = lax.all_to_all(
                expand(mixed_orbitals, sub_valence), "ka", split_axis=3, concat_axis=2, tiled=True
            )
            back = lax.all_to_all(
                spectral(sent, sub_weights, forward), "ka", split_axis=2, concat_axis=3, tiled=True
            )
            partials.append(contract(back, sub_valence))
        summed_terms = (partials[0][0] + partials[1][0], partials[0][1] + partials[1][1])
        sliced = tuple((part for part in cond_pair))
        result = complex_multiply("mkc,skmv->cksv", conjugated_rows(sliced), summed_terms)
        kernel = lax.psum_scatter(
            jnp.stack(result, axis=2), "rows", scatter_dimension=0, tiled=True
        )
        return energy * state + kernel

    first = apply(amplitudes)
    return (first, apply(first))


def solution(mesh):
    placed = (
        P("rows", "ka", None, None, None),
        P(None, "rows", "ka", None),
        P(None, "rows", "ka", None),
        P(None, None, "ka", "rows"),
        P("rows", "ka"),
        P("ka", None),
        P(),
    )

    def run(*arrays):
        vectors, rows = arrays[0].shape[3], mesh.shape["rows"]
        return spread(by_vector if vectors == rows == 2 else per_device)(*arrays)

    spread = lambda part: jax.shard_map(
        part,
        mesh=mesh,
        in_specs=placed,
        out_specs=(P("rows", "ka", None, None, None), P("rows", "ka", None, None, None)),
        check_vma=False,
    )
    return run
```
